32 devices in a mesh: groups: 2 (over x), ctx: 16 (over z, y, core).
Axes of the slice: x: 2, y: 2, z: 4, core: 2. Of those that a mesh axis runs over, the one named last changes fastest.
Arguments:
- index_query: bfloat16 [512, 8192], P(('groups', 'ctx')), parts along dimension 0, may hold values from -4 to 4
- index_weight: float32 [512, 64], P(('groups', 'ctx')), parts along dimension 0, may hold values from -0.08 to 0.08
- index_keys: bfloat16 [8192, 128], P(('groups', 'ctx')), parts along dimension 0, may hold values from -4 to 4
- attn_query: bfloat16 [512, 128, 576], P(('groups', 'ctx')), parts along dimension 0, may hold values from -80 to 80
- latent_cache: bfloat16 [8192, 576], P(('groups', 'ctx')), parts along dimension 0, may hold values from -6 to 6
- positions: int32 [512], P(('groups', 'ctx')), parts along dimension 0, may hold values from 0 to 4095, as said below
- sel_keys: int32 [512, 2048], P(('groups', 'ctx')), parts along dimension 0, may hold values from 0 to 4095, as said below
- sel_count: int32 [512], P(('groups', 'ctx')), parts along dimension 0, may hold values from 1 to 1216, as said below
- page_slot: int32 [2048], P(('groups', 'ctx')), parts along dimension 0, may hold values from 0 to 1023, as said below
Outputs:
- index_scores: float32 [512, 4096], P(('groups', 'ctx')), parts along dimension 0
- attn_latent: bfloat16 [512, 128, 512], P(('groups', 'ctx')), parts along dimension 0
- decode_latent: bfloat16 [2048, 4, 576], P(('groups', 'ctx')), parts along dimension 0
- decode_index: bfloat16 [2048, 4, 128], P(('groups', 'ctx')), parts along dimension 0
The draws below stay inside these ranges and needn't reach their ends.
There are 2 independent parts, one for each index of `groups`. The reference program is written for one: setup_inputs(seed, part) draws one part's arguments, and reference() takes and returns one part's arrays. A program takes and returns all parts, laid end to end along the dimension named above; each array names one. Nothing has to cross between parts.
Inputs may be any that keep to these rules, and one draw needn't show every extreme that they name: The 16 queries of device d sit at distinct rising positions among that device's rows d * 256 to d * 256 + 255, the last of them at the device's last row. `sel_keys`: row q lists sel_count[q] distinct rising key positions, none after positions[q] and one equal to it, then zeros. Among the keys named by the lists of one device's queries, at most 64 are rows of any one other device, and exactly 64 for some pair of devices in every draw. `sel_count`: the number of live slots in row q of sel_keys; the largest is reached in every draw. `page_slot`: A permutation. Slot s is held by device s // 64. The pages of one device go to 16 different devices, 4 to each, and every device receives 64 pages.
All inputs are finite; a program needn't handle non-finite values.
Results may differ from the reference program's by a relative error of at most 0.0047.
Values may be sent and summed in bfloat16 or wider, within the bound.
A program may use at most 128 MiB of HBM per device.

```python
import jax
import jax.numpy as jnp
from jax import lax

HEADS = 128
LAT = 512
IH = 64
IDK = 128
TOPK = 2048
CTX_DEV = 256
Q_DEV = 16
FETCH = 64
PAGE = 4
ROW = 576
QRY = 256
LEN = 4096
PAGES_DEV = 64
NPAGES = 1024
N_CTX = 16


def distinct_order(key, rows, width):
    spread = jax.random.randint(key, (rows, width), 0, 1 << 20, dtype=jnp.int32)
    return jnp.argsort(spread * width + jnp.arange(width, dtype=jnp.int32)[None, :], axis=1).astype(jnp.int32)


def shared_layout(key):
    base_key = jax.random.fold_in(key, 101)
    key_place, key_pool, key_pick = jax.random.split(base_key, 3)
    order = distinct_order(key_place, N_CTX, CTX_DEV - 1)
    offsets = jnp.sort(order[:, :Q_DEV - 1], axis=1)
    offsets = jnp.concatenate([offsets, jnp.full((N_CTX, 1), CTX_DEV - 1, jnp.int32)], axis=1)
    pool = distinct_order(key_pool, N_CTX * N_CTX, CTX_DEV)[:, :FETCH]
    pool = jnp.sort(pool, axis=1).reshape(N_CTX, N_CTX, FETCH)
    owners = jnp.arange(N_CTX, dtype=jnp.int32)
    cells = jnp.arange(CTX_DEV, dtype=jnp.int32)
    remote = owners[None, :, None] * CTX_DEV + pool
    remote_ok = jnp.broadcast_to(owners[None, :, None] < owners[:, None, None], remote.shape)
    remote_rows = jnp.repeat(remote.reshape(N_CTX, N_CTX * FETCH), Q_DEV, axis=0)
    remote_flags = jnp.repeat(remote_ok.reshape(N_CTX, N_CTX * FETCH), Q_DEV, axis=0)
    local_rows = jnp.repeat(owners[:, None] * CTX_DEV + cells[None, :], Q_DEV, axis=0)
    flat_offsets = offsets.reshape(-1)
    local_flags = cells[None, :] <= flat_offsets[:, None]
    self_flags = cells[None, :] == flat_offsets[:, None]
    width_all = N_CTX * FETCH + CTX_DEV
    candidates = jnp.concatenate([remote_rows, local_rows, jnp.zeros((QRY, TOPK), jnp.int32)], axis=1)
    columns = jnp.arange(width_all, dtype=jnp.int32)[None, :]
    random_rank = jax.random.randint(key_pick, (QRY, width_all), 0, 1 << 17, dtype=jnp.int32) * width_all + columns
    allowed = jnp.concatenate([remote_flags, local_flags], axis=1)
    selfish = jnp.concatenate([jnp.zeros((QRY, N_CTX * FETCH), bool), self_flags], axis=1)
    ranking = jnp.where(selfish, (1 << 30) + columns, jnp.where(allowed, random_rank, -1))
    ranking = jnp.concatenate([ranking, jnp.full((QRY, TOPK), -1, jnp.int32)], axis=1)
    values, picked = lax.top_k(ranking, TOPK)
    chosen = jnp.take_along_axis(candidates, picked, axis=1)
    valid = values >= 0
    chosen = jnp.sort(jnp.where(valid, chosen, LEN), axis=1)
    counts = jnp.sum(valid.astype(jnp.int32), axis=1).astype(jnp.int32)
    chosen = jnp.where(chosen == LEN, 0, chosen).astype(jnp.int32)
    places = (owners[:, None] * CTX_DEV + offsets).reshape(-1).astype(jnp.int32)
    return (places, chosen, counts)


def draw_positions(key, part):
    places, chosen, counts = shared_layout(key)
    return places


def draw_sel_keys(key, part):
    places, chosen, counts = shared_layout(key)
    return chosen


def draw_sel_count(key, part):
    places, chosen, counts = shared_layout(key)
    return counts


def draw_attn_query(key, part):
    own_key = jax.random.fold_in(key, 5)
    base = jnp.clip(jax.random.normal(own_key, (QRY, HEADS, ROW), jnp.float32), -6.0, 6.0)
    return base.astype(jnp.bfloat16)


def draw_latent_cache(key, part):
    own_key = jax.random.fold_in(key, 9)
    base = jnp.clip(jax.random.normal(own_key, (LEN, ROW), jnp.float32), -6.0, 6.0)
    return base.astype(jnp.bfloat16)


def draw_page_slot(key, part):
    key = jax.random.fold_in(key, 11)
    key_one, key_two, key_three, key_four = jax.random.split(key, 4)
    first_perm = distinct_order(key_one, 1, N_CTX)[0]
    second_perm = distinct_order(key_two, 1, N_CTX)[0]
    spread_pages = distinct_order(key_three, N_CTX, PAGES_DEV)
    within = distinct_order(key_four, N_CTX, PAGES_DEV)
    owner = first_perm[(second_perm[:, None] + spread_pages) % N_CTX]
    slot = owner * PAGES_DEV + within[owner, spread_pages]
    return slot.reshape(-1).astype(jnp.int32)


def block_scale(key, extent, cuts, least, top_value):
    level = 1.0
    for position, shards_of in cuts:
        steps = jax.random.uniform(jax.random.fold_in(jax.random.fold_in(key, 6), position), (shards_of,), jnp.float32, least / len(cuts), top_value / len(cuts))
        level = level * jnp.repeat(jnp.exp(steps), extent[position] // shards_of).reshape((-1,) + (1,) * (len(extent) - 1 - position))
    return level


def gaussian(stream_key, dims, scale, limit, pieces=(), held_as=jnp.bfloat16):
    values = jax.random.normal(stream_key, dims, jnp.float32) * scale
    if len(pieces) > 0:
        values = block_scale(stream_key, dims, pieces, -0.22, 0.18) * values
    return jnp.clip(values, min=-limit, max=limit).astype(held_as)


def setup_inputs(seed: int = 0, part: int = 0) -> dict:
    key_of = jax.random.split(jax.random.key(seed), 10)
    part_splits = jax.random.split(jax.random.fold_in(key_of[9], part), 10)
    return {
        "index_query": gaussian(part_splits[0], (QRY, IH * IDK), 1.0, 4.0, ((0, 16),)),
        "index_weight": gaussian(part_splits[1], (QRY, IH), 0.016, 0.08, ((0, 16),), jnp.float32),
        "index_keys": gaussian(part_splits[2], (LEN, IDK), 1.0, 4.0, ((0, 16),)),
        "attn_query": draw_attn_query(jax.random.fold_in(jax.random.fold_in(key_of[9], part), 71), part),
        "latent_cache": draw_latent_cache(jax.random.fold_in(jax.random.fold_in(key_of[9], part), 71), part),
        "positions": draw_positions(jax.random.fold_in(jax.random.fold_in(key_of[9], part), 71), part),
        "sel_keys": draw_sel_keys(jax.random.fold_in(jax.random.fold_in(key_of[9], part), 71), part),
        "sel_count": draw_sel_count(jax.random.fold_in(jax.random.fold_in(key_of[9], part), 71), part),
        "page_slot": draw_page_slot(jax.random.fold_in(jax.random.fold_in(key_of[9], part), 71), part),
    }


score_scale = 192.0 ** -0.5
neg_fill = -1.0e30


def reference(index_query, index_weight, index_keys, attn_query, latent_cache, positions, sel_keys, sel_count, page_slot):
    keys_wide = index_keys.astype(jnp.float32)
    blocks_query = index_query.reshape(QRY // Q_DEV, Q_DEV, IH, IDK)
    blocks_weight = index_weight.reshape(QRY // Q_DEV, Q_DEV, IH)
    blocks_place = positions.reshape(QRY // Q_DEV, Q_DEV)
    columns = jnp.arange(LEN, dtype=jnp.int32)

    def index_block(entry):
        raw = jnp.einsum("qhd,kd->qhk", entry[0].astype(jnp.float32), keys_wide, precision=lax.Precision.HIGHEST)
        summed = jnp.sum(jnp.maximum(raw, 0.0) * entry[1][:, :, None], axis=1)
        return jnp.where(columns[None, :] <= entry[2][:, None], summed, jnp.zeros_like(summed))

    index_scores = lax.map(index_block, (blocks_query, blocks_weight, blocks_place)).reshape(QRY, LEN)
    slot_ids = jnp.arange(TOPK, dtype=jnp.int32)

    def attend_entry(entry):
        gathered = latent_cache[entry[1]]
        gathered_wide = gathered.astype(jnp.float32)
        scores = jnp.dot(entry[0].astype(jnp.float32), gathered_wide.T, precision=lax.Precision.HIGHEST) * score_scale
        scores = jnp.where(slot_ids[None, :] < entry[2], scores, neg_fill)
        lifted = jnp.exp(scores - jnp.max(scores, axis=1, keepdims=True))
        shares = (lifted / jnp.sum(lifted, axis=1, keepdims=True)).astype(jnp.bfloat16)
        shares_wide = lax.optimization_barrier(shares).astype(jnp.float32)
        output = jnp.dot(shares_wide, gathered_wide[:, :LAT], precision=lax.Precision.HIGHEST)
        return output.astype(jnp.bfloat16)

    attn_latent = lax.map(attend_entry, (attn_query, sel_keys, sel_count))
    decode_latent = jnp.zeros((NPAGES, PAGE, ROW), jnp.bfloat16).at[page_slot].set(latent_cache.reshape(NPAGES, PAGE, ROW))
    decode_index = jnp.zeros((NPAGES, PAGE, IDK), jnp.bfloat16).at[page_slot].set(index_keys.reshape(NPAGES, PAGE, IDK))
    return index_scores, attn_latent, decode_latent, decode_index
```

```python
import functools
import math

import jax
import jax.numpy as jnp
from jax import lax
from jax.experimental import pallas as pl
from jax.experimental.pallas import tpu as pltpu
from jax.sharding import PartitionSpec as P

LAT = 512
PAGE = 4
FETCH = 64
LANES = 128
neg_fill = -1e30
score_scale = 192.0 ** (-0.5)
NT = (((1,), (1,)), ((), ()))


def prepare_kernel(members, local_rows, me_ref, keys_ref, count_ref, pick_ref, bias_ref, marks):
    me = me_ref[0]
    queries, slots = keys_ref.shape
    blocks = members * local_rows // LANES
    per = local_rows // LANES

    def mark(q, carry):
        keys = keys_ref[pl.ds(q, 1), :]
        live = lax.broadcasted_iota(jnp.int32, (1, slots), 1) < count_ref[q]
        keys = jnp.where(live, keys, -1)
        high = jnp.broadcast_to(keys >> 7, (blocks, slots))
        low = jnp.broadcast_to(keys & 127, (LANES, slots))
        in_block = (high == lax.broadcasted_iota(jnp.int32, (blocks, slots), 0)).astype(jnp.bfloat16)
        in_lane = (low == lax.broadcasted_iota(jnp.int32, (LANES, slots), 0)).astype(jnp.bfloat16)
        marks[:, pl.ds(q, 1), :] = lax.dot_general(
            in_block, in_lane, NT, preferred_element_type=jnp.float32
        ).reshape(blocks, 1, LANES)
        return carry

    lax.fori_loop(0, queries, mark, 0)

    def owner_marks(owner):
        return jnp.concatenate([marks[owner * per + k] for k in range(per)], axis=1)

    before = (
        lax.broadcasted_iota(jnp.int32, (local_rows, local_rows), 0)
        < lax.broadcasted_iota(jnp.int32, (local_rows, local_rows), 1)
    ).astype(jnp.bfloat16)
    place = lax.broadcasted_iota(jnp.int32, (FETCH, local_rows), 0).astype(jnp.float32)

    def compact(owner):
        own = owner_marks(owner)
        used = jnp.max(own, axis=0, keepdims=True)
        used = jnp.where(me == owner, 0.0, used)
        rank = jnp.dot(
            jnp.broadcast_to(used, (16, local_rows)).astype(jnp.bfloat16),
            before,
            preferred_element_type=jnp.float32,
        )[:1]
        rank = jnp.where(used > 0.5, rank, -1.0)
        pick = (jnp.broadcast_to(rank, (FETCH, local_rows)) == place).astype(jnp.bfloat16)
        return pick, lax.dot_general(
            own.astype(jnp.bfloat16), pick, NT, preferred_element_type=jnp.float32
        )

    for pair in range(members // 2):
        pick_a, named_a = compact(2 * pair)
        pick_b, named_b = compact(2 * pair + 1)
        pick_ref[2 * pair] = pick_a
        pick_ref[2 * pair + 1] = pick_b
        named = jnp.concatenate([named_a, named_b], axis=1)
        bias_ref[:, pair * LANES : (pair + 1) * LANES] = jnp.where(named > 0.5, 0.0, neg_fill)
    bias_ref[:, members * FETCH :] = jnp.where(owner_marks(me) > 0.5, 0.0, neg_fill)


def index_kernel(heads, query_ref, weight_ref, keys_ref, place_ref, out_ref, stacked, spread):
    queries = query_ref.shape[0]
    width = keys_ref.shape[1]
    step = 512
    for h in range(heads):
        stacked[h * queries : (h + 1) * queries, :] = query_ref[:, h * width : (h + 1) * width]
        spread[h * queries : (h + 1) * queries, :] = jnp.broadcast_to(
            weight_ref[:, h : h + 1], (queries, LANES)
        )
    places = jnp.broadcast_to(place_ref[...], (queries, step))
    group = 16

    def block(b, carry):
        start = pl.multiple_of(b * step, step)
        keys = keys_ref[pl.ds(start, step), :]
        total = jnp.zeros((queries, step), jnp.float32)
        for g in range(heads // group):
            rows = slice(g * group * queries, (g + 1) * group * queries)
            raw = lax.dot_general(stacked[rows, :], keys, NT, preferred_element_type=jnp.float32)
            raw = jnp.maximum(raw, 0.0)
            for k in range(group):
                weight = spread[(g * group + k) * queries : (g * group + k + 1) * queries, :]
                total = total + raw[k * queries : (k + 1) * queries] * jnp.concatenate(
                    [weight] * (step // LANES), axis=1
                )
        columns = start + lax.broadcasted_iota(jnp.int32, (queries, step), 1)
        out_ref[:, pl.ds(start, step)] = jnp.where(columns <= places, total, 0.0)
        return carry

    lax.fori_loop(0, keys_ref.shape[0] // step, block, 0)


def attend_kernel(
    members, group, me_ref, slot_ref, pick_ref, bias_ref, query_ref, table_ref, index_ref,
    out_ref, latent_out, index_out, chosen, onehot,
):
    me = me_ref[0]
    local_rows = table_ref.shape[0] // members
    queries, heads, row = query_ref.shape

    def bring(owner, carry):
        source = table_ref[pl.ds(pl.multiple_of(owner * local_rows, local_rows), local_rows), :]
        chosen[pl.ds(pl.multiple_of(owner * FETCH, FETCH), FETCH), :] = jnp.dot(
            pick_ref[owner], source, preferred_element_type=jnp.float32
        ).astype(jnp.bfloat16)
        return carry

    lax.fori_loop(0, members, bring, 0)
    chosen[members * FETCH :, :] = table_ref[
        pl.ds(pl.multiple_of(me * local_rows, local_rows), local_rows), :
    ]

    factor = score_scale * math.log2(math.e)

    def attend(g, carry):
        query = query_ref[pl.ds(g * group, group)].reshape(group * heads, row)
        scores = lax.dot_general(query, chosen[...], NT, preferred_element_type=jnp.float32)
        shares, sums = [], []
        for k in range(group):
            part = scores[k * heads : (k + 1) * heads] + bias_ref[pl.ds(g * group + k, 1), :]
            highest = jnp.max(part, axis=1, keepdims=True)
            lifted = jnp.exp2((part - highest) * factor)
            sums.append(jnp.sum(lifted, axis=1, keepdims=True))
            shares.append(lifted.astype(jnp.bfloat16))
        total = jnp.dot(
            jnp.concatenate(shares, axis=0), chosen[:, :LAT], preferred_element_type=jnp.float32
        )
        total = total / jnp.concatenate(sums, axis=0)
        out_ref[pl.ds(g * group, group)] = total.astype(jnp.bfloat16).reshape(group, heads, LAT)
        return carry

    lax.fori_loop(0, queries // group, attend, 0)

    target = me * local_rows + lax.broadcasted_iota(jnp.int32, (local_rows, local_rows), 0)

    def route(owner, carry):
        start = pl.multiple_of(owner * local_rows, local_rows)
        slots = jnp.broadcast_to(slot_ref[:, pl.ds(start, local_rows)], (local_rows, local_rows))
        onehot[:, pl.ds(start, local_rows)] = (slots == target).astype(jnp.bfloat16)
        return carry

    lax.fori_loop(0, members, route, 0)
    latent_out[...] = jnp.dot(
        onehot[...], table_ref[...], preferred_element_type=jnp.float32
    ).astype(jnp.bfloat16)
    index_out[...] = jnp.dot(
        onehot[...], index_ref[...], preferred_element_type=jnp.float32
    ).astype(jnp.bfloat16)


VMEM = pl.BlockSpec(memory_space=pltpu.VMEM)
SMEM = pl.BlockSpec(memory_space=pltpu.SMEM)


def on_device(
    index_query, index_weight, index_keys, attn_query, latent_cache, positions, sel_keys,
    sel_count, page_slot,
):
    members = lax.axis_size("ctx")
    local_rows, row = latent_cache.shape
    queries, index_heads = index_weight.shape
    head_width = index_keys.shape[1]
    attn_heads = attn_query.shape[1]
    total_rows = members * local_rows
    columns = members * FETCH + local_rows
    params = pltpu.CompilerParams(vmem_limit_bytes=60 * 2**20)
    me = lax.axis_index("ctx").reshape(1).astype(jnp.int32)

    row_slot = (page_slot[:, None] * PAGE + jnp.arange(PAGE, dtype=jnp.int32)[None, :]).reshape(1, -1)
    all_index = lax.all_gather(index_keys, "ctx", axis=0, tiled=True)
    table = lax.all_gather(latent_cache, "ctx", axis=0, tiled=True)
    all_slots = lax.all_gather(row_slot, "ctx", axis=1, tiled=True)

    pick, bias = pl.pallas_call(
        functools.partial(prepare_kernel, members, local_rows),
        out_shape=(
            jax.ShapeDtypeStruct((members, FETCH, local_rows), jnp.bfloat16),
            jax.ShapeDtypeStruct((queries, columns), jnp.float32),
        ),
        in_specs=[SMEM, VMEM, SMEM],
        out_specs=(VMEM, VMEM),
        scratch_shapes=[pltpu.VMEM((total_rows // LANES, queries, LANES), jnp.float32)],
        compiler_params=params,
        cost_estimate=pl.CostEstimate(flops=10**9, bytes_accessed=10**7, transcendentals=0),
        name="prepare",
    )(me, sel_keys, sel_count)

    index_scores = pl.pallas_call(
        functools.partial(index_kernel, index_heads),
        out_shape=jax.ShapeDtypeStruct((queries, total_rows), jnp.float32),
        in_specs=[VMEM] * 4,
        out_specs=VMEM,
        scratch_shapes=[
            pltpu.VMEM((index_heads * queries, head_width), jnp.bfloat16),
            pltpu.VMEM((index_heads * queries, LANES), jnp.float32),
        ],
        compiler_params=params,
        cost_estimate=pl.CostEstimate(flops=10**9, bytes_accessed=2 * 10**7, transcendentals=0),
        name="index_scores",
    )(index_query, index_weight, all_index, positions[:, None])

    attn_latent, decode_latent, decode_index = pl.pallas_call(
        functools.partial(attend_kernel, members, 4 if columns <= 2048 else 2),
        out_shape=(
            jax.ShapeDtypeStruct((queries, attn_heads, LAT), jnp.bfloat16),
            jax.ShapeDtypeStruct((local_rows, row), jnp.bfloat16),
            jax.ShapeDtypeStruct((local_rows, head_width), jnp.bfloat16),
        ),
        in_specs=[SMEM] + [VMEM] * 6,
        out_specs=(VMEM,) * 3,
        scratch_shapes=[
            pltpu.VMEM((columns, row), jnp.bfloat16),
            pltpu.VMEM((local_rows, total_rows), jnp.bfloat16),
        ],
        compiler_params=params,
        name="attend",
    )(me, all_slots, pick, bias, attn_query, table, all_index)
    return (
        index_scores,
        attn_latent,
        decode_latent.reshape(local_rows // PAGE, PAGE, row),
        decode_index.reshape(local_rows // PAGE, PAGE, head_width),
    )


def solution(mesh):
    rows = P(("groups", "ctx"), None)
    deep = P(("groups", "ctx"), None, None)
    flat = P(("groups", "ctx"))
    return jax.shard_map(
        on_device,
        mesh=mesh,
        in_specs=(rows, rows, rows, deep, rows, flat, rows, flat, flat),
        out_specs=(rows, deep, deep, deep),
        check_vma=False,
    )
```

```python
import functools
import math

import jax
import jax.numpy as jnp
from jax import lax
from jax.experimental import pallas as pl
from jax.experimental.pallas import tpu as pltpu
from jax.sharding import PartitionSpec as P

LAT = 512
PAGE = 4
FETCH = 64
LANES = 128
neg_fill = -1e30
score_scale = 192.0 ** (-0.5)
NT = (((1,), (1,)), ((), ()))


def exchange_kernel(
    members, heads, group,
    row_ref, index_ref, slot_ref, keys_ref, count_ref, query_ref, weight_ref, place_ref,
    index_out, chosen_out, bias_ref, latent_out, page_out,
    table, index_all, slot_all, marks, pick_ref, stacked, spread, latent_sum, page_sum,
    send_sem, recv_sem,
):
    me = lax.axis_index("ctx")
    core, side, depth = lax.rem(me, 2), lax.rem(me // 2, 2), members // 4
    far = me // 4
    row, local_rows = row_ref.shape
    queries, slots = keys_ref.shape
    per = local_rows // LANES
    blocks = members * per

    def at(z, y, c):
        return z * 4 + y * 2 + c

    above = at(lax.rem(far + 1, depth), side, core)
    below = at(lax.rem(far + depth - 1, depth), side, core)
    across = at(far, 1 - side, core)
    twin = at(far, side, 1 - core)
    has_above, has_below = far + 1 < depth, far > 0

    def copies(owner, target, way):
        return [
            pltpu.make_async_remote_copy(
                src_ref=ref.at[owner],
                dst_ref=ref.at[owner],
                send_sem=send_sem.at[way, kind, owner],
                recv_sem=recv_sem.at[kind, owner],
                device_id={"ctx": target},
                device_id_type=pl.DeviceIdType.MESH,
            )
            for kind, ref in enumerate((index_all, slot_all, table))
        ]

    def send(owner, target, way):
        for copy in copies(owner, target, way):
            copy.start()

    def arrived(owner):
        for copy in copies(owner, twin, 3):
            copy.wait_recv()

    table[me] = row_ref[...]
    index_all[me] = index_ref[...]
    slot_all[me] = slot_ref[...]

    barrier = pltpu.get_barrier_semaphore()

    def greet(target):
        pl.semaphore_signal(
            barrier, inc=1, device_id={"ctx": target}, device_id_type=pl.DeviceIdType.MESH
        )

    greet(across)
    greet(twin)
    pl.when(has_above)(lambda: greet(above))
    pl.when(has_below)(lambda: greet(below))
    pl.semaphore_wait(barrier, 2 + has_above.astype(jnp.int32) + has_below.astype(jnp.int32))

    send(me, across, 2)
    pl.when(has_above)(lambda: send(me, above, 0))
    pl.when(has_below)(lambda: send(me, below, 1))
    send(me, twin, 3)

    def mark(q, carry):
        keys = keys_ref[pl.ds(q, 1), :]
        live = lax.broadcasted_iota(jnp.int32, (1, slots), 1) < count_ref[q]
        keys = jnp.where(live, keys, -1)
        high = jnp.broadcast_to(keys >> 7, (blocks, slots))
        low = jnp.broadcast_to(keys & 127, (LANES, slots))
        in_block = (high == lax.broadcasted_iota(jnp.int32, (blocks, slots), 0)).astype(jnp.bfloat16)
        in_lane = (low == lax.broadcasted_iota(jnp.int32, (LANES, slots), 0)).astype(jnp.bfloat16)
        marks[:, pl.ds(q, 1), :] = lax.dot_general(
            in_block, in_lane, NT, preferred_element_type=jnp.float32
        ).reshape(blocks, 1, LANES)
        return carry

    def owner_marks(owner):
        return jnp.concatenate([marks[owner * per + k] for k in range(per)], axis=1)

    early = queries * 3 // 4

    def prepare():
        lax.fori_loop(early, queries, mark, 0)
        before = (
            lax.broadcasted_iota(jnp.int32, (local_rows, local_rows), 0)
            < lax.broadcasted_iota(jnp.int32, (local_rows, local_rows), 1)
        ).astype(jnp.bfloat16)
        place = lax.broadcasted_iota(jnp.int32, (2 * FETCH, local_rows), 0)

        def compact(owner, half):
            own = owner_marks(owner)
            used = jnp.max(own, axis=0, keepdims=True)
            used = used * jnp.where(me == owner, 0.0, 1.0)
            rank = jnp.dot(
                jnp.broadcast_to(used, (16, local_rows)).astype(jnp.bfloat16),
                before,
                preferred_element_type=jnp.float32,
            )[:1]
            rank = jnp.where(used > 0.5, rank, -1.0)
            rows = (place - half * FETCH).astype(jnp.float32)
            inside = jnp.broadcast_to(rank, (2 * FETCH, local_rows))
            pick = ((inside == rows) & (inside > -0.5)).astype(jnp.bfloat16)
            pick_ref[owner] = pick
            return lax.dot_general(
                own.astype(jnp.bfloat16), pick, NT, preferred_element_type=jnp.float32
            )

        def pair_bias(pair, carry):
            named = compact(2 * pair, 0) + compact(2 * pair + 1, 1)
            bias_ref[:, pl.ds(pl.multiple_of(pair * LANES, LANES), LANES)] = jnp.where(
                named > 0.5, 0.0, neg_fill
            )
            return carry

        lax.fori_loop(0, members // 2, pair_bias, 0)
        bias_ref[:, members * FETCH :] = jnp.where(owner_marks(me) > 0.5, 0.0, neg_fill)
        chosen_out[:, members * FETCH :] = row_ref[...]

    width = index_ref.shape[1]
    for h in range(heads):
        stacked[h * queries : (h + 1) * queries, :] = query_ref[:, h * width : (h + 1) * width]
        spread[h * queries : (h + 1) * queries, :] = jnp.broadcast_to(
            weight_ref[:, h : h + 1], (queries, LANES)
        )
    latent_sum[...] = jnp.zeros_like(latent_sum)
    page_sum[...] = jnp.zeros_like(page_sum)
    lax.fori_loop(0, early, mark, 0)

    def use(z, y):
        first = at(z, y, 0)
        named = jnp.zeros((row, 2 * FETCH), jnp.float32)
        for half in range(2):
            owner = first + half
            keys = index_all[owner]
            rows = table[owner]
            total = jnp.zeros((queries, local_rows), jnp.float32)
            for g in range(heads // group):
                part = slice(g * group * queries, (g + 1) * group * queries)
                raw = lax.dot_general(
                    stacked[part, :], keys, NT, preferred_element_type=jnp.float32
                )
                raw = jnp.maximum(raw, 0.0)
                for k in range(group):
                    weight = spread[(g * group + k) * queries : (g * group + k + 1) * queries, :]
                    total = total + raw[k * queries : (k + 1) * queries] * jnp.concatenate(
                        [weight] * per, axis=1
                    )
            start = pl.multiple_of(owner * local_rows, local_rows)
            columns = start + lax.broadcasted_iota(jnp.int32, (queries, local_rows), 1)
            places = jnp.broadcast_to(place_ref[...], (queries, local_rows))
            index_out[:, pl.ds(start, local_rows)] = jnp.where(columns <= places, total, 0.0)
            named = named + lax.dot_general(
                rows, pick_ref[owner], NT, preferred_element_type=jnp.float32
            )
            goal = me * local_rows + lax.broadcasted_iota(jnp.int32, (local_rows, local_rows), 0)
            moved = (
                jnp.broadcast_to(slot_all[owner], (local_rows, local_rows)) == goal
            ).astype(jnp.bfloat16)
            latent_sum[...] += lax.dot_general(moved, rows, NT, preferred_element_type=jnp.float32)
            page_sum[...] += jnp.dot(moved, keys, preferred_element_type=jnp.float32)
        chosen_out[:, pl.ds(pl.multiple_of(first * FETCH, 2 * FETCH), 2 * FETCH)] = named.astype(
            jnp.bfloat16
        )

    def hop(k, carry):
        @pl.when(far - k >= 0)
        def _():
            owner = at(far - k, side, core)
            arrived(owner)
            pl.when(has_above)(lambda: send(owner, above, 0))
            send(owner, across, 2)
            send(owner, twin, 3)

        @pl.when(far + k < depth)
        def _():
            owner = at(far + k, side, core)
            arrived(owner)
            pl.when(has_below)(lambda: send(owner, below, 1))
            send(owner, across, 2)
            send(owner, twin, 3)

        def from_across(z):
            owner = at(z, 1 - side, core)
            arrived(owner)
            send(owner, twin, 3)

        last = k - 1
        behind = far - last >= 0
        ahead = (far + last < depth) & (last > 0)
        pl.when(behind)(lambda: from_across(far - last))
        pl.when(ahead)(lambda: from_across(far + last))
        pl.when(last == 0)(prepare)

        def finish(z, y):
            arrived(at(z, y, 1 - core))
            use(z, y)

        def finish_all(i, carry):
            z = far + (2 * (i // 2) - 1) * last
            y = lax.rem(side + lax.rem(i, 2), 2)
            pl.when((z >= 0) & (z < depth) & ((last > 0) | (i < 2)))(lambda: finish(z, y))
            return carry

        lax.fori_loop(0, 4, finish_all, 0)
        return carry

    lax.fori_loop(1, depth + 1, hop, 0)
    latent_out[...] = latent_sum[...].astype(jnp.bfloat16)
    page_out[...] = page_sum[...].astype(jnp.bfloat16)

    def sent(owner, target, way):
        for copy in copies(owner, target, way):
            copy.wait_send()

    def drain(z, carry):
        owner = at(z, side, core)
        pl.when(has_above & (z <= far))(lambda: sent(owner, above, 0))
        pl.when(has_below & (z >= far))(lambda: sent(owner, below, 1))
        sent(owner, across, 2)
        sent(owner, twin, 3)
        sent(at(z, 1 - side, core), twin, 3)
        return carry

    lax.fori_loop(0, depth, drain, 0)


def attend_kernel(bias_ref, query_ref, chosen_ref, out_ref):
    group, row, heads = query_ref.shape
    factor = score_scale * math.log2(math.e)
    first = pl.program_id(0) * group
    query = jnp.concatenate([query_ref[k].T for k in range(group)], axis=0)
    scores = jnp.dot(query, chosen_ref[...], preferred_element_type=jnp.float32)
    shares, sums = [], []
    for k in range(group):
        part = scores[k * heads : (k + 1) * heads] + bias_ref[pl.ds(first + k, 1), :]
        highest = jnp.max(part, axis=1, keepdims=True)
        lifted = jnp.exp2((part - highest) * factor)
        sums.append(jnp.sum(lifted, axis=1, keepdims=True))
        shares.append(lifted.astype(jnp.bfloat16))
    total = lax.dot_general(
        jnp.concatenate(shares, axis=0), chosen_ref[:LAT, :], NT, preferred_element_type=jnp.float32
    )
    total = total / jnp.concatenate(sums, axis=0)
    out_ref[...] = total.astype(jnp.bfloat16).reshape(group, heads, LAT)


VMEM = pl.BlockSpec(memory_space=pltpu.VMEM)
SMEM = pl.BlockSpec(memory_space=pltpu.SMEM)


def on_device(
    index_query, index_weight, index_keys, attn_query, latent_cache, positions, sel_keys,
    sel_count, page_slot,
):
    members = lax.axis_size("ctx")
    local_rows, row = latent_cache.shape
    queries, index_heads = index_weight.shape
    head_width = index_keys.shape[1]
    attn_heads = attn_query.shape[1]
    total_rows = members * local_rows
    columns = members * FETCH + local_rows
    row_slot = (page_slot[:, None] * PAGE + jnp.arange(PAGE, dtype=jnp.int32)[None, :]).reshape(1, -1)

    index_scores, chosen, bias, decode_latent, decode_index = pl.pallas_call(
        functools.partial(exchange_kernel, members, index_heads, 16),
        out_shape=(
            jax.ShapeDtypeStruct((queries, total_rows), jnp.float32),
            jax.ShapeDtypeStruct((row, columns), jnp.bfloat16),
            jax.ShapeDtypeStruct((queries, columns), jnp.float32),
            jax.ShapeDtypeStruct((local_rows, row), jnp.bfloat16),
            jax.ShapeDtypeStruct((local_rows, head_width), jnp.bfloat16),
        ),
        in_specs=[VMEM] * 4 + [SMEM] + [VMEM] * 3,
        out_specs=(VMEM,) * 5,
        scratch_shapes=[
            pltpu.VMEM((members, row, local_rows), jnp.bfloat16),
            pltpu.VMEM((members, local_rows, head_width), jnp.bfloat16),
            pltpu.VMEM((members, 1, local_rows), jnp.int32),
            pltpu.VMEM((total_rows // LANES, queries, LANES), jnp.float32),
            pltpu.VMEM((members, 2 * FETCH, local_rows), jnp.bfloat16),
            pltpu.VMEM((index_heads * queries, head_width), jnp.bfloat16),
            pltpu.VMEM((index_heads * queries, LANES), jnp.float32),
            pltpu.VMEM((local_rows, row), jnp.float32),
            pltpu.VMEM((local_rows, head_width), jnp.float32),
            pltpu.SemaphoreType.DMA((4, 3, members)),
            pltpu.SemaphoreType.DMA((3, members)),
        ],
        compiler_params=pltpu.CompilerParams(
            collective_id=0, has_side_effects=True, vmem_limit_bytes=60 * 2**20
        ),
        name="exchange",
    )(
        latent_cache.T, index_keys, row_slot, sel_keys, sel_count, index_query, index_weight,
        positions[:, None],
    )

    group = 4 if columns <= 2048 else 2
    attn_latent = pl.pallas_call(
        attend_kernel,
        grid=(queries // group,),
        out_shape=jax.ShapeDtypeStruct((queries, attn_heads, LAT), jnp.bfloat16),
        in_specs=[
            pl.BlockSpec((queries, columns), lambda g: (0, 0)),
            pl.BlockSpec((group, row, attn_heads), lambda g: (g, 0, 0)),
            pl.BlockSpec((row, columns), lambda g: (0, 0)),
        ],
        out_specs=pl.BlockSpec((group, attn_heads, LAT), lambda g: (g, 0, 0)),
        compiler_params=pltpu.CompilerParams(vmem_limit_bytes=60 * 2**20),
        name="attend",
    )(bias, jnp.swapaxes(attn_query, 1, 2), chosen)
    return (
        index_scores,
        attn_latent,
        decode_latent.reshape(local_rows // PAGE, PAGE, row),
        decode_index.reshape(local_rows // PAGE, PAGE, head_width),
    )


def solution(mesh):
    rows = P(("groups", "ctx"), None)
    deep = P(("groups", "ctx"), None, None)
    flat = P(("groups", "ctx"))
    return jax.shard_map(
        on_device,
        mesh=mesh,
        in_specs=(rows, rows, rows, deep, rows, flat, rows, flat, flat),
        out_specs=(rows, deep, deep, deep),
        check_vma=False,
    )
```

```python
import functools
import math

import jax
import jax.numpy as jnp
from jax import lax
from jax.experimental import pallas as pl
from jax.experimental.pallas import tpu as pltpu
from jax.sharding import PartitionSpec as P

LAT = 512
PAGE = 4
FETCH = 64
LANES = 128
neg_fill = -1e30
score_scale = 192.0 ** (-0.5)
NT = (((1,), (1,)), ((), ()))


def exchange_kernel(
    members, heads, group,
    row_ref, index_ref, slot_ref, keys_ref, count_ref, query_ref, weight_ref, place_ref,
    index_out, chosen_out, bias_ref, latent_sum, page_sum,
    table, index_all, slot_all, marks, pick_ref, stacked, spread, places_all,
    send_sem, recv_sem,
):
    me = lax.axis_index("ctx")
    core, side, depth = lax.rem(me, 2), lax.rem(me // 2, 2), members // 4
    far = me // 4
    row, local_rows = row_ref.shape
    queries, slots = keys_ref.shape
    per = local_rows // LANES
    blocks = members * per

    def at(z, y, c):
        return z * 4 + y * 2 + c

    above = at(lax.rem(far + 1, depth), side, core)
    below = at(lax.rem(far + depth - 1, depth), side, core)
    across = at(far, 1 - side, core)
    twin = at(far, side, 1 - core)
    has_above, has_below = far + 1 < depth, far > 0

    def copies(owner, target, way):
        return [
            pltpu.make_async_remote_copy(
                src_ref=ref.at[owner],
                dst_ref=ref.at[owner],
                send_sem=send_sem.at[way, kind, owner],
                recv_sem=recv_sem.at[kind, owner],
                device_id={"ctx": target},
                device_id_type=pl.DeviceIdType.MESH,
            )
            for kind, ref in enumerate((index_all, slot_all, table))
        ]

    def send(owner, target, way):
        for copy in copies(owner, target, way):
            copy.start()

    def arrived(owner):
        for copy in copies(owner, twin, 3):
            copy.wait_recv()

    table[me] = row_ref[...]
    index_all[me] = index_ref[...]
    pages = slot_ref.shape[1]
    fine = lax.broadcasted_iota(jnp.int32, (pages, local_rows), 1)
    spread_pages = (
        (fine // PAGE) == lax.broadcasted_iota(jnp.int32, (pages, local_rows), 0)
    ).astype(jnp.bfloat16)

    def widen(values):
        values = jnp.broadcast_to(values.astype(jnp.float32), (16, pages)).astype(jnp.bfloat16)
        return jnp.dot(values, spread_pages, preferred_element_type=jnp.float32)[:1]

    slot = widen(slot_ref[...] >> 6) * 64.0 + widen(slot_ref[...] & 63)
    slot_all[me] = slot.astype(jnp.int32) * PAGE + fine[:1] % PAGE

    barrier = pltpu.get_barrier_semaphore()

    def greet(target):
        pl.semaphore_signal(
            barrier, inc=1, device_id={"ctx": target}, device_id_type=pl.DeviceIdType.MESH
        )

    greet(across)
    greet(twin)
    pl.when(has_above)(lambda: greet(above))
    pl.when(has_below)(lambda: greet(below))
    pl.semaphore_wait(barrier, 2 + has_above.astype(jnp.int32) + has_below.astype(jnp.int32))

    send(me, across, 2)
    pl.when(has_above)(lambda: send(me, above, 0))
    pl.when(has_below)(lambda: send(me, below, 1))
    send(me, twin, 3)

    def mark(q, carry):
        keys = keys_ref[pl.ds(q, 1), :]
        live = lax.broadcasted_iota(jnp.int32, (1, slots), 1) < count_ref[q]
        keys = jnp.where(live, keys, -1)
        high = jnp.broadcast_to(keys >> 7, (blocks, slots))
        low = jnp.broadcast_to(keys & 127, (LANES, slots))
        in_block = (high == lax.broadcasted_iota(jnp.int32, (blocks, slots), 0)).astype(jnp.bfloat16)
        in_lane = (low == lax.broadcasted_iota(jnp.int32, (LANES, slots), 0)).astype(jnp.bfloat16)
        marks[:, pl.ds(q, 1), :] = lax.dot_general(
            in_block, in_lane, NT, preferred_element_type=jnp.float32
        ).reshape(blocks, 1, LANES)
        return carry

    def owner_marks(owner):
        return jnp.concatenate([marks[owner * per + k] for k in range(per)], axis=1)

    early = queries * 3 // 4

    def prepare():
        lax.fori_loop(early, queries, mark, 0)
        before = (
            lax.broadcasted_iota(jnp.int32, (local_rows, local_rows), 0)
            < lax.broadcasted_iota(jnp.int32, (local_rows, local_rows), 1)
        ).astype(jnp.bfloat16)
        place = lax.broadcasted_iota(jnp.int32, (2 * FETCH, local_rows), 0)

        def compact(owner, half):
            own = owner_marks(owner)
            used = jnp.max(own, axis=0, keepdims=True)
            used = used * jnp.where(me == owner, 0.0, 1.0)
            rank = jnp.dot(
                jnp.broadcast_to(used, (16, local_rows)).astype(jnp.bfloat16),
                before,
                preferred_element_type=jnp.float32,
            )[:1]
            rank = jnp.where(used > 0.5, rank, -1.0)
            rows = (place - half * FETCH).astype(jnp.float32)
            inside = jnp.broadcast_to(rank, (2 * FETCH, local_rows))
            pick = ((inside == rows) & (inside > -0.5)).astype(jnp.bfloat16)
            pick_ref[owner] = pick
            return lax.dot_general(
                own.astype(jnp.bfloat16), pick, NT, preferred_element_type=jnp.float32
            )

        def pair_bias(pair, carry):
            named = compact(2 * pair, 0) + compact(2 * pair + 1, 1)
            bias_ref[:, pl.ds(pl.multiple_of(pair * LANES, LANES), LANES)] = jnp.where(
                named > 0.5, 0.0, neg_fill
            )
            return carry

        lax.fori_loop(0, members // 2, pair_bias, 0)
        bias_ref[:, members * FETCH :] = jnp.where(owner_marks(me) > 0.5, 0.0, neg_fill)
        chosen_out[:, members * FETCH :] = row_ref[...]

    width = index_ref.shape[1]
    for h in range(heads):
        stacked[h * queries : (h + 1) * queries, :] = query_ref[:, h * width : (h + 1) * width]
        spread[h * queries : (h + 1) * queries, :] = jnp.broadcast_to(
            weight_ref[:, h : h + 1], (queries, LANES)
        )
    seat = lax.broadcasted_iota(jnp.int32, (queries, LANES), 0)
    places_here = jnp.zeros((queries, LANES), jnp.int32)
    for q in range(queries):
        places_here = jnp.where(seat == q, place_ref[q], places_here)
    places_all[...] = places_here
    latent_sum[...] = jnp.zeros_like(latent_sum)
    page_sum[...] = jnp.zeros_like(page_sum)
    lax.fori_loop(0, early, mark, 0)

    def use(z, y):
        first = at(z, y, 0)
        named = jnp.zeros((row, 2 * FETCH), jnp.float32)
        for half in range(2):
            owner = first + half
            keys = index_all[owner]
            rows = table[owner]
            total = jnp.zeros((queries, local_rows), jnp.float32)
            for g in range(heads // group):
                part = slice(g * group * queries, (g + 1) * group * queries)
                raw = lax.dot_general(
                    stacked[part, :], keys, NT, preferred_element_type=jnp.float32
                )
                raw = jnp.maximum(raw, 0.0)
                for k in range(group):
                    weight = spread[(g * group + k) * queries : (g * group + k + 1) * queries, :]
                    total = total + raw[k * queries : (k + 1) * queries] * jnp.concatenate(
                        [weight] * per, axis=1
                    )
            start = pl.multiple_of(owner * local_rows, local_rows)
            columns = start + lax.broadcasted_iota(jnp.int32, (queries, local_rows), 1)
            places = jnp.concatenate([places_all[...]] * per, axis=1)
            index_out[:, pl.ds(start, local_rows)] = jnp.where(columns <= places, total, 0.0)
            named = named + lax.dot_general(
                rows, pick_ref[owner], NT, preferred_element_type=jnp.float32
            )
            goal = me * local_rows + lax.broadcasted_iota(jnp.int32, (local_rows, local_rows), 0)
            moved = (
                jnp.broadcast_to(slot_all[owner], (local_rows, local_rows)) == goal
            ).astype(jnp.bfloat16)
            latent_sum[...] += lax.dot_general(moved, rows, NT, preferred_element_type=jnp.float32)
            page_sum[...] += jnp.dot(moved, keys, preferred_element_type=jnp.float32)
        chosen_out[:, pl.ds(pl.multiple_of(first * FETCH, 2 * FETCH), 2 * FETCH)] = named.astype(
            jnp.bfloat16
        )

    def hop(k, carry):
        @pl.when(far - k >= 0)
        def _():
            owner = at(far - k, side, core)
            arrived(owner)
            pl.when(has_above)(lambda: send(owner, above, 0))
            send(owner, across, 2)
            send(owner, twin, 3)

        @pl.when(far + k < depth)
        def _():
            owner = at(far + k, side, core)
            arrived(owner)
            pl.when(has_below)(lambda: send(owner, below, 1))
            send(owner, across, 2)
            send(owner, twin, 3)

        def from_across(z):
            owner = at(z, 1 - side, core)
            arrived(owner)
            send(owner, twin, 3)

        last = k - 1
        behind = far - last >= 0
        ahead = (far + last < depth) & (last > 0)
        pl.when(behind)(lambda: from_across(far - last))
        pl.when(ahead)(lambda: from_across(far + last))
        pl.when(last == 0)(prepare)

        def finish(z, y):
            arrived(at(z, y, 1 - core))
            use(z, y)

        def finish_all(i, carry):
            z = far + (2 * (i // 2) - 1) * last
            y = lax.rem(side + lax.rem(i, 2), 2)
            pl.when((z >= 0) & (z < depth) & ((last > 0) | (i < 2)))(lambda: finish(z, y))
            return carry

        lax.fori_loop(0, 4, finish_all, 0)
        return carry

    lax.fori_loop(1, depth + 1, hop, 0)

    def sent(owner, target, way):
        for copy in copies(owner, target, way):
            copy.wait_send()

    def drain(z, carry):
        owner = at(z, side, core)
        pl.when(has_above & (z <= far))(lambda: sent(owner, above, 0))
        pl.when(has_below & (z >= far))(lambda: sent(owner, below, 1))
        sent(owner, across, 2)
        sent(owner, twin, 3)
        sent(at(z, 1 - side, core), twin, 3)
        return carry

    lax.fori_loop(0, depth, drain, 0)


def attend_kernel(
    bias_ref, query_ref, chosen_ref, scores_ref, latent_ref, page_ref,
    out_ref, scores_out, latent_out, page_out,
):
    group, row, heads = query_ref.shape
    scores_out[...] = scores_ref[...]
    for page in range(latent_out.shape[0]):
        latent_out[page] = latent_ref[page * PAGE : (page + 1) * PAGE, :].astype(jnp.bfloat16)
        page_out[page] = page_ref[page * PAGE : (page + 1) * PAGE, :].astype(jnp.bfloat16)
    factor = score_scale * math.log2(math.e)
    first = pl.program_id(0) * group
    query = jnp.concatenate([query_ref[k].T for k in range(group)], axis=0)
    scores = jnp.dot(query, chosen_ref[...], preferred_element_type=jnp.float32)
    shares, sums = [], []
    for k in range(group):
        part = scores[k * heads : (k + 1) * heads] + bias_ref[pl.ds(first + k, 1), :]
        highest = jnp.max(part, axis=1, keepdims=True)
        lifted = jnp.exp2((part - highest) * factor)
        sums.append(jnp.sum(lifted, axis=1, keepdims=True))
        shares.append(lifted.astype(jnp.bfloat16))
    total = lax.dot_general(
        jnp.concatenate(shares, axis=0), chosen_ref[:LAT, :], NT, preferred_element_type=jnp.float32
    )
    total = total / jnp.concatenate(sums, axis=0)
    out_ref[...] = total.astype(jnp.bfloat16).reshape(group, heads, LAT)


VMEM = pl.BlockSpec(memory_space=pltpu.VMEM)
SMEM = pl.BlockSpec(memory_space=pltpu.SMEM)


def on_device(
    index_query, index_weight, index_keys, attn_query, latent_cache, positions, sel_keys,
    sel_count, page_slot,
):
    members = lax.axis_size("ctx")
    local_rows, row = latent_cache.shape
    queries, index_heads = index_weight.shape
    head_width = index_keys.shape[1]
    attn_heads = attn_query.shape[1]
    total_rows = members * local_rows
    columns = members * FETCH + local_rows

    scores, chosen, bias, decode_latent, decode_index = pl.pallas_call(
        functools.partial(exchange_kernel, members, index_heads, 16),
        out_shape=(
            jax.ShapeDtypeStruct((queries, total_rows), jnp.float32),
            jax.ShapeDtypeStruct((row, columns), jnp.bfloat16),
            jax.ShapeDtypeStruct((queries, columns), jnp.float32),
            jax.ShapeDtypeStruct((local_rows, row), jnp.float32),
            jax.ShapeDtypeStruct((local_rows, head_width), jnp.float32),
        ),
        in_specs=[VMEM] * 4 + [SMEM] + [VMEM] * 2 + [SMEM],
        out_specs=(VMEM,) * 5,
        scratch_shapes=[
            pltpu.VMEM((members, row, local_rows), jnp.bfloat16),
            pltpu.VMEM((members, local_rows, head_width), jnp.bfloat16),
            pltpu.VMEM((members, 1, local_rows), jnp.int32),
            pltpu.VMEM((total_rows // LANES, queries, LANES), jnp.float32),
            pltpu.VMEM((members, 2 * FETCH, local_rows), jnp.bfloat16),
            pltpu.VMEM((index_heads * queries, head_width), jnp.bfloat16),
            pltpu.VMEM((index_heads * queries, LANES), jnp.float32),
            pltpu.VMEM((queries, LANES), jnp.int32),
            pltpu.SemaphoreType.DMA((4, 3, members)),
            pltpu.SemaphoreType.DMA((3, members)),
        ],
        compiler_params=pltpu.CompilerParams(
            collective_id=0, has_side_effects=True, vmem_limit_bytes=60 * 2**20
        ),
        name="exchange",
    )(
        latent_cache.T, index_keys, page_slot.reshape(1, -1), sel_keys, sel_count, index_query,
        index_weight, positions,
    )

    group = 4 if columns <= 2048 else 2
    steps = queries // group
    pages = local_rows // PAGE
    attn_latent, index_scores, decode_latent, decode_index = pl.pallas_call(
        attend_kernel,
        grid=(steps,),
        out_shape=(
            jax.ShapeDtypeStruct((queries, attn_heads, LAT), jnp.bfloat16),
            jax.ShapeDtypeStruct((queries, total_rows), jnp.float32),
            jax.ShapeDtypeStruct((pages, PAGE, row), jnp.bfloat16),
            jax.ShapeDtypeStruct((pages, PAGE, head_width), jnp.bfloat16),
        ),
        in_specs=[
            pl.BlockSpec((queries, columns), lambda g: (0, 0)),
            pl.BlockSpec((group, row, attn_heads), lambda g: (g, 0, 0)),
            pl.BlockSpec((row, columns), lambda g: (0, 0)),
            pl.BlockSpec((queries, total_rows // steps), lambda g: (0, g)),
            pl.BlockSpec((local_rows // steps, row), lambda g: (g, 0)),
            pl.BlockSpec((local_rows // steps, head_width), lambda g: (g, 0)),
        ],
        out_specs=(
            pl.BlockSpec((group, attn_heads, LAT), lambda g: (g, 0, 0)),
            pl.BlockSpec((queries, total_rows // steps), lambda g: (0, g)),
            pl.BlockSpec((pages // steps, PAGE, row), lambda g: (g, 0, 0)),
            pl.BlockSpec((pages // steps, PAGE, head_width), lambda g: (g, 0, 0)),
        ),
        compiler_params=pltpu.CompilerParams(vmem_limit_bytes=60 * 2**20),
        name="attend",
    )(bias, jnp.swapaxes(attn_query, 1, 2), chosen, scores, decode_latent, decode_index)
    return index_scores, attn_latent, decode_latent, decode_index


def solution(mesh):
    rows = P(("groups", "ctx"), None)
    deep = P(("groups", "ctx"), None, None)
    flat = P(("groups", "ctx"))
    return jax.shard_map(
        on_device,
        mesh=mesh,
        in_specs=(rows, rows, rows, deep, rows, flat, rows, flat, flat),
        out_specs=(rows, deep, deep, deep),
        check_vma=False,
    )
```

```python
import functools
import math

import jax
import jax.numpy as jnp
from jax import lax
from jax.experimental import pallas as pl
from jax.experimental.pallas import tpu as pltpu
from jax.sharding import PartitionSpec as P

LAT = 512
PAGE = 4
FETCH = 64
LANES = 128
neg_fill = -1e30
score_scale = 192.0 ** (-0.5)
NT = (((1,), (1,)), ((), ()))


def exchange_kernel(
    members, heads, group,
    row_ref, index_ref, slot_ref, keys_ref, count_ref, query_ref, weight_ref, place_ref,
    index_out, chosen_out, bias_ref, latent_sum, page_sum,
    table, index_all, slot_all, marks, pick_ref, stacked, spread, places_all,
    send_sem, recv_sem,
):
    me = lax.axis_index("ctx")
    core, side, depth = lax.rem(me, 2), lax.rem(me // 2, 2), members // 4
    far = me // 4
    row, local_rows = row_ref.shape
    queries, slots = keys_ref.shape
    per = local_rows // LANES
    blocks = members * per

    def at(z, y, c):
        return z * 4 + y * 2 + c

    above = at(lax.rem(far + 1, depth), side, core)
    below = at(lax.rem(far + depth - 1, depth), side, core)
    across = at(far, 1 - side, core)
    twin = at(far, side, 1 - core)
    has_above, has_below = far + 1 < depth, far > 0

    def early_cross(z):
        return (core == 0) & ((z == 0) | (z == depth - 1))

    def copies(owner, target, way):
        return [
            pltpu.make_async_remote_copy(
                src_ref=ref.at[owner],
                dst_ref=ref.at[owner],
                send_sem=send_sem.at[way, kind, owner],
                recv_sem=recv_sem.at[kind, owner],
                device_id={"ctx": target},
                device_id_type=pl.DeviceIdType.MESH,
            )
            for kind, ref in enumerate((index_all, slot_all, table))
        ]

    def send(owner, target, way):
        for copy in copies(owner, target, way):
            copy.start()

    def arrived(owner):
        for copy in copies(owner, twin, 3):
            copy.wait_recv()

    table[me] = row_ref[...]
    index_all[me] = index_ref[...]
    pages = slot_ref.shape[1]
    fine = lax.broadcasted_iota(jnp.int32, (pages, local_rows), 1)
    spread_pages = (
        (fine // PAGE) == lax.broadcasted_iota(jnp.int32, (pages, local_rows), 0)
    ).astype(jnp.bfloat16)

    def widen(values):
        values = jnp.broadcast_to(values.astype(jnp.float32), (16, pages)).astype(jnp.bfloat16)
        return jnp.dot(values, spread_pages, preferred_element_type=jnp.float32)[:1]

    slot = widen(slot_ref[...] >> 6) * 64.0 + widen(slot_ref[...] & 63)
    slot_all[me] = slot.astype(jnp.int32) * PAGE + fine[:1] % PAGE

    barrier = pltpu.get_barrier_semaphore()

    def greet(target):
        pl.semaphore_signal(
            barrier, inc=1, device_id={"ctx": target}, device_id_type=pl.DeviceIdType.MESH
        )

    greet(across)
    greet(twin)
    pl.when(has_above)(lambda: greet(above))
    pl.when(has_below)(lambda: greet(below))
    pl.semaphore_wait(barrier, 2 + has_above.astype(jnp.int32) + has_below.astype(jnp.int32))

    send(me, across, 2)
    pl.when(has_above)(lambda: send(me, above, 0))
    pl.when(has_below)(lambda: send(me, below, 1))
    send(me, twin, 3)

    def mark(q, carry):
        keys = keys_ref[pl.ds(q, 1), :]
        live = lax.broadcasted_iota(jnp.int32, (1, slots), 1) < count_ref[q]
        keys = jnp.where(live, keys, -1)
        high = jnp.broadcast_to(keys >> 7, (blocks, slots))
        low = jnp.broadcast_to(keys & 127, (LANES, slots))
        in_block = (high == lax.broadcasted_iota(jnp.int32, (blocks, slots), 0)).astype(jnp.bfloat16)
        in_lane = (low == lax.broadcasted_iota(jnp.int32, (LANES, slots), 0)).astype(jnp.bfloat16)
        marks[:, pl.ds(q, 1), :] = lax.dot_general(
            in_block, in_lane, NT, preferred_element_type=jnp.float32
        ).reshape(blocks, 1, LANES)
        return carry

    def owner_marks(owner):
        return jnp.concatenate([marks[owner * per + k] for k in range(per)], axis=1)

    early = queries * 3 // 4

    def prepare():
        lax.fori_loop(early, queries, mark, 0)
        before = (
            lax.broadcasted_iota(jnp.int32, (local_rows, local_rows), 0)
            < lax.broadcasted_iota(jnp.int32, (local_rows, local_rows), 1)
        ).astype(jnp.bfloat16)
        place = lax.broadcasted_iota(jnp.int32, (2 * FETCH, local_rows), 0)

        def compact(owner, half):
            own = owner_marks(owner)
            used = jnp.max(own, axis=0, keepdims=True)
            used = used * jnp.where(me == owner, 0.0, 1.0)
            rank = jnp.dot(
                jnp.broadcast_to(used, (16, local_rows)).astype(jnp.bfloat16),
                before,
                preferred_element_type=jnp.float32,
            )[:1]
            rank = jnp.where(used > 0.5, rank, -1.0)
            rows = (place - half * FETCH).astype(jnp.float32)
            inside = jnp.broadcast_to(rank, (2 * FETCH, local_rows))
            pick = ((inside == rows) & (inside > -0.5)).astype(jnp.bfloat16)
            pick_ref[owner] = pick
            return lax.dot_general(
                own.astype(jnp.bfloat16), pick, NT, preferred_element_type=jnp.float32
            )

        def pair_bias(pair, carry):
            named = compact(2 * pair, 0) + compact(2 * pair + 1, 1)
            bias_ref[:, pl.ds(pl.multiple_of(pair * LANES, LANES), LANES)] = jnp.where(
                named > 0.5, 0.0, neg_fill
            )
            return carry

        lax.fori_loop(0, members // 2, pair_bias, 0)
        bias_ref[:, members * FETCH :] = jnp.where(owner_marks(me) > 0.5, 0.0, neg_fill)
        chosen_out[:, members * FETCH :] = row_ref[...]

    width = index_ref.shape[1]
    for h in range(heads):
        stacked[h * queries : (h + 1) * queries, :] = query_ref[:, h * width : (h + 1) * width]
        spread[h * queries : (h + 1) * queries, :] = jnp.broadcast_to(
            weight_ref[:, h : h + 1], (queries, LANES)
        )
    seat = lax.broadcasted_iota(jnp.int32, (queries, LANES), 0)
    places_here = jnp.zeros((queries, LANES), jnp.int32)
    for q in range(queries):
        places_here = jnp.where(seat == q, place_ref[q], places_here)
    places_all[...] = places_here
    latent_sum[...] = jnp.zeros_like(latent_sum)
    page_sum[...] = jnp.zeros_like(page_sum)
    lax.fori_loop(0, early, mark, 0)

    def use(z, y):
        first = at(z, y, 0)
        named = jnp.zeros((row, 2 * FETCH), jnp.float32)
        for half in range(2):
            owner = first + half
            keys = index_all[owner]
            rows = table[owner]
            total = jnp.zeros((queries, local_rows), jnp.float32)
            for g in range(heads // group):
                part = slice(g * group * queries, (g + 1) * group * queries)
                raw = lax.dot_general(
                    stacked[part, :], keys, NT, preferred_element_type=jnp.float32
                )
                raw = jnp.maximum(raw, 0.0)
                for k in range(group):
                    weight = spread[(g * group + k) * queries : (g * group + k + 1) * queries, :]
                    total = total + raw[k * queries : (k + 1) * queries] * jnp.concatenate(
                        [weight] * per, axis=1
                    )
            start = pl.multiple_of(owner * local_rows, local_rows)
            columns = start + lax.broadcasted_iota(jnp.int32, (queries, local_rows), 1)
            places = jnp.concatenate([places_all[...]] * per, axis=1)
            index_out[:, pl.ds(start, local_rows)] = jnp.where(columns <= places, total, 0.0)
            named = named + lax.dot_general(
                rows, pick_ref[owner], NT, preferred_element_type=jnp.float32
            )
            goal = me * local_rows + lax.broadcasted_iota(jnp.int32, (local_rows, local_rows), 0)
            moved = (
                jnp.broadcast_to(slot_all[owner], (local_rows, local_rows)) == goal
            ).astype(jnp.bfloat16)
            latent_sum[...] += lax.dot_general(moved, rows, NT, preferred_element_type=jnp.float32)
            page_sum[...] += jnp.dot(moved, keys, preferred_element_type=jnp.float32)
        chosen_out[:, pl.ds(pl.multiple_of(first * FETCH, 2 * FETCH), 2 * FETCH)] = named.astype(
            jnp.bfloat16
        )

    def hop(k, carry):
        @pl.when(far - k >= 0)
        def _():
            owner = at(far - k, side, core)
            arrived(owner)
            pl.when(has_above)(lambda: send(owner, above, 0))
            pl.when(jnp.logical_not(early_cross(far - k)))(lambda: send(owner, across, 2))
            send(owner, twin, 3)

        @pl.when(far + k < depth)
        def _():
            owner = at(far + k, side, core)
            arrived(owner)
            pl.when(has_below)(lambda: send(owner, below, 1))
            pl.when(jnp.logical_not(early_cross(far + k)))(lambda: send(owner, across, 2))
            send(owner, twin, 3)

        def from_across(z):
            owner = at(z, 1 - side, core)
            arrived(owner)
            pl.when(early_cross(z) & has_above & (z <= far))(lambda: send(owner, above, 0))
            pl.when(early_cross(z) & has_below & (z >= far))(lambda: send(owner, below, 1))
            send(owner, twin, 3)

        last = k - 1
        behind = far - last >= 0
        ahead = (far + last < depth) & (last > 0)
        pl.when(behind)(lambda: from_across(far - last))
        pl.when(ahead)(lambda: from_across(far + last))
        pl.when(last == 0)(prepare)

        def finish(z, y):
            arrived(at(z, y, 1 - core))
            use(z, y)

        def finish_all(i, carry):
            z = far + (2 * (i // 2) - 1) * last
            y = lax.rem(side + lax.rem(i, 2), 2)
            pl.when((z >= 0) & (z < depth) & ((last > 0) | (i < 2)))(lambda: finish(z, y))
            return carry

        lax.fori_loop(0, 4, finish_all, 0)
        return carry

    lax.fori_loop(1, depth + 1, hop, 0)

    def sent(owner, target, way):
        for copy in copies(owner, target, way):
            copy.wait_send()

    def drain(z, carry):
        owner = at(z, side, core)
        pl.when(has_above & (z <= far))(lambda: sent(owner, above, 0))
        pl.when(has_below & (z >= far))(lambda: sent(owner, below, 1))
        pl.when((z == far) | jnp.logical_not(early_cross(z)))(lambda: sent(owner, across, 2))
        sent(owner, twin, 3)
        other = at(z, 1 - side, core)
        pl.when(early_cross(z) & has_above & (z <= far))(lambda: sent(other, above, 0))
        pl.when(early_cross(z) & has_below & (z >= far))(lambda: sent(other, below, 1))
        sent(other, twin, 3)
        return carry

    lax.fori_loop(0, depth, drain, 0)


def attend_kernel(
    bias_ref, query_ref, chosen_ref, scores_ref, latent_ref, page_ref,
    out_ref, scores_out, latent_out, page_out,
):
    group, row, heads = query_ref.shape
    scores_out[...] = scores_ref[...]
    for page in range(latent_out.shape[0]):
        latent_out[page] = latent_ref[page * PAGE : (page + 1) * PAGE, :].astype(jnp.bfloat16)
        page_out[page] = page_ref[page * PAGE : (page + 1) * PAGE, :].astype(jnp.bfloat16)
    factor = score_scale * math.log2(math.e)
    first = pl.program_id(0) * group
    query = jnp.concatenate([query_ref[k].T for k in range(group)], axis=0)
    scores = jnp.dot(query, chosen_ref[...], preferred_element_type=jnp.float32)
    shares, sums = [], []
    for k in range(group):
        part = scores[k * heads : (k + 1) * heads] + bias_ref[pl.ds(first + k, 1), :]
        highest = jnp.max(part, axis=1, keepdims=True)
        lifted = jnp.exp2((part - highest) * factor)
        sums.append(jnp.sum(lifted, axis=1, keepdims=True))
        shares.append(lifted.astype(jnp.bfloat16))
    total = lax.dot_general(
        jnp.concatenate(shares, axis=0), chosen_ref[:LAT, :], NT, preferred_element_type=jnp.float32
    )
    total = total / jnp.concatenate(sums, axis=0)
    out_ref[...] = total.astype(jnp.bfloat16).reshape(group, heads, LAT)


VMEM = pl.BlockSpec(memory_space=pltpu.VMEM)
SMEM = pl.BlockSpec(memory_space=pltpu.SMEM)


def on_device(
    index_query, index_weight, index_keys, attn_query, latent_cache, positions, sel_keys,
    sel_count, page_slot,
):
    members = lax.axis_size("ctx")
    local_rows, row = latent_cache.shape
    queries, index_heads = index_weight.shape
    head_width = index_keys.shape[1]
    attn_heads = attn_query.shape[1]
    total_rows = members * local_rows
    columns = members * FETCH + local_rows

    scores, chosen, bias, decode_latent, decode_index = pl.pallas_call(
        functools.partial(exchange_kernel, members, index_heads, 16),
        out_shape=(
            jax.ShapeDtypeStruct((queries, total_rows), jnp.float32),
            jax.ShapeDtypeStruct((row, columns), jnp.bfloat16),
            jax.ShapeDtypeStruct((queries, columns), jnp.float32),
            jax.ShapeDtypeStruct((local_rows, row), jnp.float32),
            jax.ShapeDtypeStruct((local_rows, head_width), jnp.float32),
        ),
        in_specs=[VMEM] * 4 + [SMEM] + [VMEM] * 2 + [SMEM],
        out_specs=(VMEM,) * 5,
        scratch_shapes=[
            pltpu.VMEM((members, row, local_rows), jnp.bfloat16),
            pltpu.VMEM((members, local_rows, head_width), jnp.bfloat16),
            pltpu.VMEM((members, 1, local_rows), jnp.int32),
            pltpu.VMEM((total_rows // LANES, queries, LANES), jnp.float32),
            pltpu.VMEM((members, 2 * FETCH, local_rows), jnp.bfloat16),
            pltpu.VMEM((index_heads * queries, head_width), jnp.bfloat16),
            pltpu.VMEM((index_heads * queries, LANES), jnp.float32),
            pltpu.VMEM((queries, LANES), jnp.int32),
            pltpu.SemaphoreType.DMA((4, 3, members)),
            pltpu.SemaphoreType.DMA((3, members)),
        ],
        compiler_params=pltpu.CompilerParams(
            collective_id=0, has_side_effects=True, vmem_limit_bytes=60 * 2**20
        ),
        name="exchange",
    )(
        latent_cache.T, index_keys, page_slot.reshape(1, -1), sel_keys, sel_count, index_query,
        index_weight, positions,
    )

    group = 4 if columns <= 2048 else 2
    steps = queries // group
    pages = local_rows // PAGE
    attn_latent, index_scores, decode_latent, decode_index = pl.pallas_call(
        attend_kernel,
        grid=(steps,),
        out_shape=(
            jax.ShapeDtypeStruct((queries, attn_heads, LAT), jnp.bfloat16),
            jax.ShapeDtypeStruct((queries, total_rows), jnp.float32),
            jax.ShapeDtypeStruct((pages, PAGE, row), jnp.bfloat16),
            jax.ShapeDtypeStruct((pages, PAGE, head_width), jnp.bfloat16),
        ),
        in_specs=[
            pl.BlockSpec((queries, columns), lambda g: (0, 0)),
            pl.BlockSpec((group, row, attn_heads), lambda g: (g, 0, 0)),
            pl.BlockSpec((row, columns), lambda g: (0, 0)),
            pl.BlockSpec((queries, total_rows // steps), lambda g: (0, g)),
            pl.BlockSpec((local_rows // steps, row), lambda g: (g, 0)),
            pl.BlockSpec((local_rows // steps, head_width), lambda g: (g, 0)),
        ],
        out_specs=(
            pl.BlockSpec((group, attn_heads, LAT), lambda g: (g, 0, 0)),
            pl.BlockSpec((queries, total_rows // steps), lambda g: (0, g)),
            pl.BlockSpec((pages // steps, PAGE, row), lambda g: (g, 0, 0)),
            pl.BlockSpec((pages // steps, PAGE, head_width), lambda g: (g, 0, 0)),
        ),
        compiler_params=pltpu.CompilerParams(vmem_limit_bytes=60 * 2**20),
        name="attend",
    )(bias, jnp.swapaxes(attn_query, 1, 2), chosen, scores, decode_latent, decode_index)
    return index_scores, attn_latent, decode_latent, decode_index


def solution(mesh):
    rows = P(("groups", "ctx"), None)
    deep = P(("groups", "ctx"), None, None)
    flat = P(("groups", "ctx"))
    return jax.shard_map(
        on_device,
        mesh=mesh,
        in_specs=(rows, rows, rows, deep, rows, flat, rows, flat, flat),
        out_specs=(rows, deep, deep, deep),
        check_vma=False,
    )
```

```python
import functools
import math

import jax
import jax.numpy as jnp
from jax import lax
from jax.experimental import pallas as pl
from jax.experimental.pallas import tpu as pltpu
from jax.sharding import PartitionSpec as P

LAT = 512
PAGE = 4
FETCH = 64
LANES = 128
neg_fill = -1e30
score_scale = 192.0 ** (-0.5)
NT = (((1,), (1,)), ((), ()))


def exchange_kernel(
    members, heads, group,
    row_ref, index_ref, slot_ref, keys_ref, count_ref, query_ref, weight_ref, place_ref,
    index_out, chosen_out, bias_ref, latent_sum, page_sum,
    table, index_all, slot_all, marks, pick_ref, stacked, spread, places_all,
    send_sem, recv_sem,
):
    me = lax.axis_index("ctx")
    core, side, depth = lax.rem(me, 2), lax.rem(me // 2, 2), members // 4
    far = me // 4
    row, local_rows = row_ref.shape
    queries, slots = keys_ref.shape
    per = local_rows // LANES
    blocks = members * per

    def at(z, y, c):
        return z * 4 + y * 2 + c

    above = at(lax.rem(far + 1, depth), side, core)
    below = at(lax.rem(far + depth - 1, depth), side, core)
    across = at(far, 1 - side, core)
    twin = at(far, side, 1 - core)
    has_above, has_below = far + 1 < depth, far > 0

    def early_cross(z):
        return (core == 0) & ((z == 0) | (z == depth - 1))

    half = row // 2

    def piece(kind, owner):
        if kind < 2:
            return (index_all, slot_all)[kind].at[owner]
        return table.at[owner, pl.ds((kind - 2) * half, half), :]

    def copy_of(kind, owner, target, way):
        return pltpu.make_async_remote_copy(
            src_ref=piece(kind, owner),
            dst_ref=piece(kind, owner),
            send_sem=send_sem.at[way, kind, owner],
            recv_sem=recv_sem.at[kind, owner],
            device_id={"ctx": target},
            device_id_type=pl.DeviceIdType.MESH,
        )

    def copies(owner, target, way):
        return [copy_of(kind, owner, target, way) for kind in range(4)]

    def send(owner, target, way):
        for copy in copies(owner, target, way):
            copy.start()

    def arrived(owner):
        for copy in copies(owner, twin, 3):
            copy.wait_recv()

    def relay(owner, routes):
        for kind in range(4):
            copy_of(kind, owner, twin, 3).wait_recv()
            for condition, target, way in routes:
                @pl.when(condition)
                def _():
                    copy_of(kind, owner, target, way).start()

            copy_of(kind, owner, twin, 3).start()

    table[me] = row_ref[...]
    index_all[me] = index_ref[...]
    pages = slot_ref.shape[1]
    fine = lax.broadcasted_iota(jnp.int32, (pages, local_rows), 1)
    spread_pages = (
        (fine // PAGE) == lax.broadcasted_iota(jnp.int32, (pages, local_rows), 0)
    ).astype(jnp.bfloat16)

    def widen(values):
        values = jnp.broadcast_to(values.astype(jnp.float32), (16, pages)).astype(jnp.bfloat16)
        return jnp.dot(values, spread_pages, preferred_element_type=jnp.float32)[:1]

    slot = widen(slot_ref[...] >> 6) * 64.0 + widen(slot_ref[...] & 63)
    slot_all[me] = slot.astype(jnp.int32) * PAGE + fine[:1] % PAGE

    barrier = pltpu.get_barrier_semaphore()

    def greet(target):
        pl.semaphore_signal(
            barrier, inc=1, device_id={"ctx": target}, device_id_type=pl.DeviceIdType.MESH
        )

    greet(across)
    greet(twin)
    pl.when(has_above)(lambda: greet(above))
    pl.when(has_below)(lambda: greet(below))
    pl.semaphore_wait(barrier, 2 + has_above.astype(jnp.int32) + has_below.astype(jnp.int32))

    send(me, across, 2)
    pl.when(has_above)(lambda: send(me, above, 0))
    pl.when(has_below)(lambda: send(me, below, 1))
    send(me, twin, 3)

    def mark(q, carry):
        keys = keys_ref[pl.ds(q, 1), :]
        live = lax.broadcasted_iota(jnp.int32, (1, slots), 1) < count_ref[q]
        keys = jnp.where(live, keys, -1)
        high = jnp.broadcast_to(keys >> 7, (blocks, slots))
        low = jnp.broadcast_to(keys & 127, (LANES, slots))
        in_block = (high == lax.broadcasted_iota(jnp.int32, (blocks, slots), 0)).astype(jnp.bfloat16)
        in_lane = (low == lax.broadcasted_iota(jnp.int32, (LANES, slots), 0)).astype(jnp.bfloat16)
        marks[:, pl.ds(q, 1), :] = lax.dot_general(
            in_block, in_lane, NT, preferred_element_type=jnp.float32
        ).reshape(blocks, 1, LANES)
        return carry

    def owner_marks(owner):
        return jnp.concatenate([marks[owner * per + k] for k in range(per)], axis=1)

    early = queries * 3 // 4

    def prepare():
        lax.fori_loop(early, queries, mark, 0)
        before = (
            lax.broadcasted_iota(jnp.int32, (local_rows, local_rows), 0)
            < lax.broadcasted_iota(jnp.int32, (local_rows, local_rows), 1)
        ).astype(jnp.bfloat16)
        place = lax.broadcasted_iota(jnp.int32, (2 * FETCH, local_rows), 0)

        def compact(owner, half):
            own = owner_marks(owner)
            used = jnp.max(own, axis=0, keepdims=True)
            used = used * jnp.where(me == owner, 0.0, 1.0)
            rank = jnp.dot(
                jnp.broadcast_to(used, (16, local_rows)).astype(jnp.bfloat16),
                before,
                preferred_element_type=jnp.float32,
            )[:1]
            rank = jnp.where(used > 0.5, rank, -1.0)
            rows = (place - half * FETCH).astype(jnp.float32)
            inside = jnp.broadcast_to(rank, (2 * FETCH, local_rows))
            pick = ((inside == rows) & (inside > -0.5)).astype(jnp.bfloat16)
            pick_ref[owner] = pick
            return lax.dot_general(
                own.astype(jnp.bfloat16), pick, NT, preferred_element_type=jnp.float32
            )

        def pair_bias(pair, carry):
            named = compact(2 * pair, 0) + compact(2 * pair + 1, 1)
            bias_ref[:, pl.ds(pl.multiple_of(pair * LANES, LANES), LANES)] = jnp.where(
                named > 0.5, 0.0, neg_fill
            )
            return carry

        lax.fori_loop(0, members // 2, pair_bias, 0)
        bias_ref[:, members * FETCH :] = jnp.where(owner_marks(me) > 0.5, 0.0, neg_fill)
        chosen_out[:, members * FETCH :] = row_ref[...]

    width = index_ref.shape[1]
    for h in range(heads):
        stacked[h * queries : (h + 1) * queries, :] = query_ref[:, h * width : (h + 1) * width]
        spread[h * queries : (h + 1) * queries, :] = jnp.broadcast_to(
            weight_ref[:, h : h + 1], (queries, LANES)
        )
    seat = lax.broadcasted_iota(jnp.int32, (queries, LANES), 0)
    places_here = jnp.zeros((queries, LANES), jnp.int32)
    for q in range(queries):
        places_here = jnp.where(seat == q, place_ref[q], places_here)
    places_all[...] = places_here
    latent_sum[...] = jnp.zeros_like(latent_sum)
    page_sum[...] = jnp.zeros_like(page_sum)
    lax.fori_loop(0, early, mark, 0)

    def use(z, y):
        first = at(z, y, 0)
        named = jnp.zeros((row, 2 * FETCH), jnp.float32)
        for half in range(2):
            owner = first + half
            keys = index_all[owner]
            rows = table[owner]
            total = jnp.zeros((queries, local_rows), jnp.float32)
            for g in range(heads // group):
                part = slice(g * group * queries, (g + 1) * group * queries)
                raw = lax.dot_general(
                    stacked[part, :], keys, NT, preferred_element_type=jnp.float32
                )
                raw = jnp.maximum(raw, 0.0)
                for k in range(group):
                    weight = spread[(g * group + k) * queries : (g * group + k + 1) * queries, :]
                    total = total + raw[k * queries : (k + 1) * queries] * jnp.concatenate(
                        [weight] * per, axis=1
                    )
            start = pl.multiple_of(owner * local_rows, local_rows)
            columns = start + lax.broadcasted_iota(jnp.int32, (queries, local_rows), 1)
            places = jnp.concatenate([places_all[...]] * per, axis=1)
            index_out[:, pl.ds(start, local_rows)] = jnp.where(columns <= places, total, 0.0)
            named = named + lax.dot_general(
                rows, pick_ref[owner], NT, preferred_element_type=jnp.float32
            )
            goal = me * local_rows + lax.broadcasted_iota(jnp.int32, (local_rows, local_rows), 0)
            moved = (
                jnp.broadcast_to(slot_all[owner], (local_rows, local_rows)) == goal
            ).astype(jnp.bfloat16)
            latent_sum[...] += lax.dot_general(moved, rows, NT, preferred_element_type=jnp.float32)
            page_sum[...] += jnp.dot(moved, keys, preferred_element_type=jnp.float32)
        chosen_out[:, pl.ds(pl.multiple_of(first * FETCH, 2 * FETCH), 2 * FETCH)] = named.astype(
            jnp.bfloat16
        )

    def hop(k, carry):
        @pl.when(far - k >= 0)
        def _():
            owner = at(far - k, side, core)
            relay(
                owner,
                ((has_above, above, 0), (jnp.logical_not(early_cross(far - k)), across, 2)),
            )

        @pl.when(far + k < depth)
        def _():
            owner = at(far + k, side, core)
            relay(
                owner,
                ((has_below, below, 1), (jnp.logical_not(early_cross(far + k)), across, 2)),
            )

        def from_across(z):
            owner = at(z, 1 - side, core)
            relay(
                owner,
                (
                    (early_cross(z) & has_above & (z <= far), above, 0),
                    (early_cross(z) & has_below & (z >= far), below, 1),
                ),
            )

        last = k - 1
        behind = far - last >= 0
        ahead = (far + last < depth) & (last > 0)
        pl.when(behind)(lambda: from_across(far - last))
        pl.when(ahead)(lambda: from_across(far + last))
        pl.when(last == 0)(prepare)

        def finish(z, y):
            arrived(at(z, y, 1 - core))
            use(z, y)

        def finish_all(i, carry):
            z = far + (2 * (i // 2) - 1) * last
            y = lax.rem(side + lax.rem(i, 2), 2)
            pl.when((z >= 0) & (z < depth) & ((last > 0) | (i < 2)))(lambda: finish(z, y))
            return carry

        lax.fori_loop(0, 4, finish_all, 0)
        return carry

    lax.fori_loop(1, depth + 1, hop, 0)

    def sent(owner, target, way):
        for copy in copies(owner, target, way):
            copy.wait_send()

    def drain(z, carry):
        owner = at(z, side, core)
        pl.when(has_above & (z <= far))(lambda: sent(owner, above, 0))
        pl.when(has_below & (z >= far))(lambda: sent(owner, below, 1))
        pl.when((z == far) | jnp.logical_not(early_cross(z)))(lambda: sent(owner, across, 2))
        sent(owner, twin, 3)
        other = at(z, 1 - side, core)
        pl.when(early_cross(z) & has_above & (z <= far))(lambda: sent(other, above, 0))
        pl.when(early_cross(z) & has_below & (z >= far))(lambda: sent(other, below, 1))
        sent(other, twin, 3)
        return carry

    lax.fori_loop(0, depth, drain, 0)


def attend_kernel(
    bias_ref, query_ref, chosen_ref, scores_ref, latent_ref, page_ref,
    out_ref, scores_out, latent_out, page_out,
):
    group, row, heads = query_ref.shape
    scores_out[...] = scores_ref[...]
    for page in range(latent_out.shape[0]):
        latent_out[page] = latent_ref[page * PAGE : (page + 1) * PAGE, :].astype(jnp.bfloat16)
        page_out[page] = page_ref[page * PAGE : (page + 1) * PAGE, :].astype(jnp.bfloat16)
    factor = score_scale * math.log2(math.e)
    first = pl.program_id(0) * group
    query = jnp.concatenate([query_ref[k].T for k in range(group)], axis=0)
    scores = jnp.dot(query, chosen_ref[...], preferred_element_type=jnp.float32)
    shares, sums = [], []
    for k in range(group):
        part = scores[k * heads : (k + 1) * heads] + bias_ref[pl.ds(first + k, 1), :]
        highest = jnp.max(part, axis=1, keepdims=True)
        lifted = jnp.exp2((part - highest) * factor)
        sums.append(jnp.sum(lifted, axis=1, keepdims=True))
        shares.append(lifted.astype(jnp.bfloat16))
    total = lax.dot_general(
        jnp.concatenate(shares, axis=0), chosen_ref[:LAT, :], NT, preferred_element_type=jnp.float32
    )
    total = total / jnp.concatenate(sums, axis=0)
    out_ref[...] = total.astype(jnp.bfloat16).reshape(group, heads, LAT)


VMEM = pl.BlockSpec(memory_space=pltpu.VMEM)
SMEM = pl.BlockSpec(memory_space=pltpu.SMEM)


def on_device(
    index_query, index_weight, index_keys, attn_query, latent_cache, positions, sel_keys,
    sel_count, page_slot,
):
    members = lax.axis_size("ctx")
    local_rows, row = latent_cache.shape
    queries, index_heads = index_weight.shape
    head_width = index_keys.shape[1]
    attn_heads = attn_query.shape[1]
    total_rows = members * local_rows
    columns = members * FETCH + local_rows

    scores, chosen, bias, decode_latent, decode_index = pl.pallas_call(
        functools.partial(exchange_kernel, members, index_heads, 16),
        out_shape=(
            jax.ShapeDtypeStruct((queries, total_rows), jnp.float32),
            jax.ShapeDtypeStruct((row, columns), jnp.bfloat16),
            jax.ShapeDtypeStruct((queries, columns), jnp.float32),
            jax.ShapeDtypeStruct((local_rows, row), jnp.float32),
            jax.ShapeDtypeStruct((local_rows, head_width), jnp.float32),
        ),
        in_specs=[VMEM] * 4 + [SMEM] + [VMEM] * 2 + [SMEM],
        out_specs=(VMEM,) * 5,
        scratch_shapes=[
            pltpu.VMEM((members, row, local_rows), jnp.bfloat16),
            pltpu.VMEM((members, local_rows, head_width), jnp.bfloat16),
            pltpu.VMEM((members, 1, local_rows), jnp.int32),
            pltpu.VMEM((total_rows // LANES, queries, LANES), jnp.float32),
            pltpu.VMEM((members, 2 * FETCH, local_rows), jnp.bfloat16),
            pltpu.VMEM((index_heads * queries, head_width), jnp.bfloat16),
            pltpu.VMEM((index_heads * queries, LANES), jnp.float32),
            pltpu.VMEM((queries, LANES), jnp.int32),
            pltpu.SemaphoreType.DMA((4, 4, members)),
            pltpu.SemaphoreType.DMA((4, members)),
        ],
        compiler_params=pltpu.CompilerParams(
            collective_id=0, has_side_effects=True, vmem_limit_bytes=60 * 2**20
        ),
        name="exchange",
    )(
        latent_cache.T, index_keys, page_slot.reshape(1, -1), sel_keys, sel_count, index_query,
        index_weight, positions,
    )

    group = 4 if columns <= 2048 else 2
    steps = queries // group
    pages = local_rows // PAGE
    attn_latent, index_scores, decode_latent, decode_index = pl.pallas_call(
        attend_kernel,
        grid=(steps,),
        out_shape=(
            jax.ShapeDtypeStruct((queries, attn_heads, LAT), jnp.bfloat16),
            jax.ShapeDtypeStruct((queries, total_rows), jnp.float32),
            jax.ShapeDtypeStruct((pages, PAGE, row), jnp.bfloat16),
            jax.ShapeDtypeStruct((pages, PAGE, head_width), jnp.bfloat16),
        ),
        in_specs=[
            pl.BlockSpec((queries, columns), lambda g: (0, 0)),
            pl.BlockSpec((group, row, attn_heads), lambda g: (g, 0, 0)),
            pl.BlockSpec((row, columns), lambda g: (0, 0)),
            pl.BlockSpec((queries, total_rows // steps), lambda g: (0, g)),
            pl.BlockSpec((local_rows // steps, row), lambda g: (g, 0)),
            pl.BlockSpec((local_rows // steps, head_width), lambda g: (g, 0)),
        ],
        out_specs=(
            pl.BlockSpec((group, attn_heads, LAT), lambda g: (g, 0, 0)),
            pl.BlockSpec((queries, total_rows // steps), lambda g: (0, g)),
            pl.BlockSpec((pages // steps, PAGE, row), lambda g: (g, 0, 0)),
            pl.BlockSpec((pages // steps, PAGE, head_width), lambda g: (g, 0, 0)),
        ),
        compiler_params=pltpu.CompilerParams(vmem_limit_bytes=60 * 2**20),
        name="attend",
    )(bias, jnp.swapaxes(attn_query, 1, 2), chosen, scores, decode_latent, decode_index)
    return index_scores, attn_latent, decode_latent, decode_index


def solution(mesh):
    rows = P(("groups", "ctx"), None)
    deep = P(("groups", "ctx"), None, None)
    flat = P(("groups", "ctx"))
    return jax.shard_map(
        on_device,
        mesh=mesh,
        in_specs=(rows, rows, rows, deep, rows, flat, rows, flat, flat),
        out_specs=(rows, deep, deep, deep),
        check_vma=False,
    )
```
